256 devices in a mesh: segment: 32 (over z, x_lo, core), fsdp: 8 (over y, x_hi).
Axes of the slice: x: 4 (x_hi: 2, x_lo: 2; x = x_hi * 2 + x_lo), y: 4, z: 8, core: 2. Of those that a mesh axis runs over, the one named last changes fastest.
Arguments:
- new_batches: bfloat16 [3, 128, 4096], P(None, 'fsdp'), may hold values from -6 to 6
- down_state: bfloat16 [32, 128, 4096], P('segment', 'fsdp'), may hold values from -6 to 6
- up_state: bfloat16 [32, 128, 4096], P('segment', 'fsdp'), may hold values from -6 to 6
- gains: float32 [32, 2, 4096], P('segment'), may hold values from 0.1 to 1.9
- w_value: bfloat16 [32, 2, 4096, 1024], P('segment', None, None, 'fsdp'), may hold values from -0.09375 to 0.09375
- w_out: bfloat16 [32, 2, 1024, 4096], P('segment', None, 'fsdp'), may hold values from -0.1875 to 0.1875
- final_gain: float32 [4096], replicated, may hold values from 0.1 to 1.9
- lm_head: bfloat16 [4096, 131072], P(None, ('segment', 'fsdp')), may hold values from -12 to 12
- teacher_logits: bfloat16 [384, 131072], P(None, ('segment', 'fsdp')), may hold values from -100 to 300
Outputs:
- down_final: bfloat16 [32, 128, 4096], P('segment', 'fsdp')
- up_final: bfloat16 [32, 128, 4096], P('segment', 'fsdp')
- student_logits: bfloat16 [384, 131072], P(None, ('segment', 'fsdp'))
- divergence: float32 [384], replicated
The draws below stay inside these ranges and needn't reach their ends.
All inputs are finite; a program needn't handle non-finite values.
Results may differ from the reference program's by a relative error of at most 0.028.
Values may be sent and summed in bfloat16 or wider, within the bound.
A program may use at most 64 MiB of HBM per device.

```python
import jax
import jax.numpy as jnp
from jax import lax

D = 4096
H = 1024
V = 131072
MB = 128
TICKS = 3
DONE = 384
N_SEGMENT = 32
N_FSDP = 8


def draw_lm_head(key, part):
    key = jax.random.fold_in(key, 11)
    base_key = jax.random.fold_in(key, 0)
    base = jnp.clip(jax.random.normal(base_key, (D, V), jnp.float32), -6.0, 6.0) * (3.0 * D ** (-0.5))
    return base.astype(jnp.bfloat16)


def draw_teacher_logits(key, part):
    key = jax.random.fold_in(key, 23)
    base_key = jax.random.fold_in(key, 0)
    base = jnp.clip(jax.random.normal(base_key, (DONE, V), jnp.float32), -6.0, 6.0) * 3.0
    return base.astype(jnp.bfloat16)


def block_scale(stream_key, dims, cuts, least, largest):
    loudness = 1.0
    for position, parts in cuts:
        heights = jax.random.uniform(jax.random.fold_in(jax.random.fold_in(stream_key, 6), position), (parts,), jnp.float32, least / len(cuts), largest / len(cuts))
        loudness = loudness * jnp.repeat(jnp.exp(heights), dims[position] // parts).reshape((-1,) + (1,) * (len(dims) - 1 - position))
    return loudness


def gaussian(rng, shape, deviation, reach, shards=(), kind=jnp.bfloat16):
    entries = jax.random.normal(rng, shape, jnp.float32) * deviation
    if len(shards) > 0:
        entries = block_scale(rng, shape, shards, -0.22, 0.18) * entries
    return jnp.clip(entries, min=-reach, max=reach).astype(kind)


def setup_inputs(seed: int = 0) -> dict:
    keys = jax.random.split(jax.random.key(seed), 10)
    new_batches = gaussian(keys[0], (TICKS, MB, D), 1.0, 6.0, ((1, 8),))
    down_state = gaussian(keys[1], (N_SEGMENT, MB, D), 1.0, 6.0, ((0, 32), (1, 8)))
    up_state = gaussian(keys[2], (N_SEGMENT, MB, D), 1.0, 6.0, ((0, 32), (1, 8)))
    gains = jnp.clip(1.0 + 0.18 * jax.random.normal(keys[3], (N_SEGMENT, 2, D), jnp.float32), 0.1, 1.9)
    w_value = gaussian(keys[4], (N_SEGMENT, 2, D, H), D ** -0.5, 0.09375, ((0, 32), (3, 8)))
    w_out = gaussian(keys[5], (N_SEGMENT, 2, H, D), H ** -0.5, 0.1875, ((0, 32), (2, 8)))
    final_gain = jnp.clip(1.0 + 0.18 * jax.random.normal(keys[6], (D,), jnp.float32), 0.1, 1.9)
    lm_head = draw_lm_head(jax.random.fold_in(keys[9], 71), 0)
    teacher_logits = draw_teacher_logits(jax.random.fold_in(keys[9], 71), 0)
    return {"new_batches": new_batches, "down_state": down_state, "up_state": up_state, "gains": gains, "w_value": w_value, "w_out": w_out, "final_gain": final_gain, "lm_head": lm_head, "teacher_logits": teacher_logits}


epsilon = 1e-06

def rms_scale(values, gain_row):
    return values * lax.rsqrt(lax.optimization_barrier(jnp.mean(values * values, axis=-1, keepdims=True)) + epsilon) * gain_row

def section(inputs, gain_row, value_proj, out_proj):
    widened = inputs.astype(jnp.float32)
    normed = rms_scale(widened, gain_row.astype(jnp.float32)).astype(jnp.bfloat16)
    head_values = jnp.dot(normed, value_proj, preferred_element_type=jnp.float32).astype(jnp.bfloat16)
    groups = head_values.reshape(head_values.shape[0], N_FSDP, H // N_FSDP).astype(jnp.float32)
    blocks = out_proj.reshape(N_FSDP, H // N_FSDP, D).astype(jnp.float32)
    partial_value = jnp.einsum('mfh,fhd->fmd', groups, blocks).astype(jnp.bfloat16)
    partial_value = lax.optimization_barrier(partial_value).astype(jnp.float32)
    return (widened + lax.optimization_barrier(jnp.sum(partial_value, axis=0))).astype(jnp.bfloat16)

def reference(new_batches, down_state, up_state, gains, w_value, w_out, final_gain, lm_head, teacher_logits):
    down_rows = down_state
    up_rows = up_state
    finished = []

    def apply_both(operands):
        down_one, up_one, gain_pair, value_pair, out_pair = operands
        return (section(down_one, gain_pair[0], value_pair[0], out_pair[0]), section(up_one, gain_pair[1], value_pair[1], out_pair[1]))
    for tick_index in range(TICKS):
        out_down, out_up = lax.map(apply_both, (down_rows, up_rows, gains, w_value, w_out))
        down_rows = jnp.concatenate([new_batches[tick_index][None], out_down[:-1]], axis=0)
        up_rows = jnp.concatenate([out_up[1:], out_down[-1:]], axis=0)
        finished.append(out_up[0])
    stacked = jnp.concatenate(finished, axis=0)
    hidden = rms_scale(stacked.astype(jnp.float32), final_gain.astype(jnp.float32)).astype(jnp.bfloat16)
    logits = jnp.dot(hidden, lm_head, preferred_element_type=jnp.float32)
    teacher = teacher_logits.astype(jnp.float32)
    teach_log = jax.nn.log_softmax(teacher, axis=-1)
    stud_log = jax.nn.log_softmax(logits, axis=-1)
    divergence = lax.optimization_barrier(jnp.sum(jnp.exp(teach_log) * (teach_log - stud_log), axis=-1))
    return (down_rows, up_rows, logits.astype(jnp.bfloat16), divergence)
```

```python
import functools

import jax
import jax.numpy as jnp
from jax import lax
from jax.experimental import pallas as pl
from jax.experimental.pallas import tpu as pltpu
from jax.sharding import PartitionSpec as P

MESH = pl.DeviceIdType.MESH
BF = jnp.bfloat16
F32 = jnp.float32
EPS = 1e-06

D = 4096
H = 1024
FS = 8
SEG = 32
MB = 128
TICKS = 3
ROWS = MB // FS
COLS = D // FS
WIDE = H + 128
VOC = 512
DOWN, UP = 0, 1
VMEM_LIMIT = 64 * 1024 * 1024 - 65536

(SEND_DOWN, SEND_UP, HEAD, REDUCE, OUT, FORWARD, SHARE, LOGITS, MERGE, FINISH, SPREAD, NOTHING) = range(12)


def step(kind, section=0, tick=0):
    return kind * 8 + section * 4 + tick


def parse(words):
    names = {
        "W": SEND_DOWN, "V": SEND_UP, "A": HEAD, "B": REDUCE, "C": OUT, "D": FORWARD, "E": SHARE,
        "F": LOGITS, "G": MERGE, "H": FINISH, "I": SPREAD,
    }
    steps = []
    for word in words:
        section, tick = 0, 0
        for mark in word[1:]:
            if mark in "du":
                section = "du".index(mark)
            else:
                tick = int(mark)
        steps.append((names[word[0]], section, tick))
    return steps


FIRST = (
    "Vu0", "Au0", "Vu1", "Vu2", "Vu3", "Wd0", "Bu0", "Wd1", "Cd0", "D0", "Cu0", "Au1",
    "Wd2", "Wd3", "Bu1", "Wu0", "Cd1", "D1", "Cu1", "Au2", "Wu1", "Wu2", "Bu2", "Wu3",
    "Ad0", "Cd2", "D2", "Ad1", "E0", "Bd0", "Bd1", "F0", "Ad2", "E1", "Bd2", "F1",
    "Cu2", "Iu", "Id", "E2", "F2", "G0", "G1", "G2", "H0", "H1", "H2",
)
MIDDLE = (
    "Vu0", "Au0", "Vu1", "Vu2", "Vu3", "Wd0", "Bu0", "Wd1", "Cu0", "Au1", "Wd2", "Wd3",
    "Bu1", "Wu0", "Wu1", "Wu2", "Wu3", "D0", "Ad0", "E0", "Bd0", "D1", "Cd0", "Ad1",
    "Cu1", "Au2", "E1", "F0", "Bd1", "Bu2", "D2", "Cd1", "Ad2", "Cu2", "E2", "F1",
    "Bd2", "F2", "Cd2", "Iu", "Id", "G0", "G1", "G2", "H0", "H1", "H2",
)
LAST = (
    "Vu0", "Au0", "Vu1", "Vu2", "Vu3", "Wd0", "Bu0", "Wd1", "Wd2", "Wd3", "Wu0", "Wu1",
    "Wu2", "Wu3", "D0", "Ad0", "E0", "Bd0", "Cu0", "Au1", "D1", "Cd0", "Ad1", "Bu1",
    "E1", "Bd1", "Cu1", "Au2", "F0", "Cd1", "Ad2", "Bu2", "Bd2", "D2", "F1", "Cu2",
    "Iu", "E2", "Cd2", "Id", "F2", "G0", "G1", "G2", "H0", "H1", "H2",
)
TABLES = [parse(FIRST), parse(MIDDLE), parse(LAST)]
STEPS = max(len(table) for table in TABLES)
TABLES = [table + [(NOTHING, 0, 0)] * (STEPS - len(table)) for table in TABLES]


def take(ref, sem):
    pltpu.make_async_copy(ref, ref, sem).wait()


def kernel(
    new_ref, down_ref, up_ref, gain_ref, value_ref, out_ref, final_ref, head_ref, teach_ref,
    down_out, up_out, logit_out, div_out,
    pw, ow, xb, xp, part, parts, hvo, hv, xo, hid, hn, acc, head, teach, cols, st1, st2, fin,
    gain, final, local_w, local_x, local_h,
    w_s, w_r, x_s, x_r, rs_s, rs_r, ag_s, ag_r, hop_s, hop_r, z_s, z_r, pl_s, pl_r, d2_s, d2_r,
    s1_s, s1_r, s2_s, s2_r, f_s, f_r,
):
    s = lax.axis_index("segment")
    f = lax.axis_index("fsdp")
    z, xl, c = lax.div(s, 4), lax.rem(lax.div(s, 2), 2), lax.rem(s, 2)
    y, xh = lax.div(f, 2), lax.rem(f, 2)
    x = xh * 2 + xl
    first, last = s == 0, s == SEG - 1
    frow = pl.multiple_of(f * ROWS, ROWS)
    fcol = pl.multiple_of(f * COLS, COLS)
    fhead = pl.multiple_of(f * 128, 128)
    quarter = c * 2 + xl
    qrow = pl.multiple_of(quarter * 32, 32)
    orow = pl.multiple_of((c * 2 + 1 - xl) * 32, 32)
    crow = pl.multiple_of(c * 64, 64)
    prow = pl.multiple_of((1 - c) * 64, 64)

    def follows(section):
        inside = jnp.where(section == DOWN, last, first)
        ahead = jnp.where(section == DOWN, 1, -1)
        return inside, s + jnp.where(inside, 0, ahead), jnp.where(inside, 1 - section, section)

    def plane(k):
        x2, y2 = lax.rem(x + lax.rem(k, 4), 4), lax.rem(y + lax.div(k, 4), 4)
        return x2, (z * 4 + lax.rem(x2, 2) * 2 + c, y2 * 2 + lax.div(x2, 2))

    def pillar(k):
        z2, c2 = lax.rem(z + lax.div(k, 2), 8), lax.rem(c + lax.rem(k, 2), 2)
        return (z2 * 4 + xl * 2 + c2, f)

    def put(src, dst, send, recv, target):
        pltpu.make_async_remote_copy(
            src_ref=src, dst_ref=dst, send_sem=send, recv_sem=recv,
            device_id=target, device_id_type=MESH,
        ).start()

    head_copy = pltpu.make_async_copy(head_ref, head, local_h.at[0])
    teach_copy = pltpu.make_async_copy(teach_ref, teach, local_h.at[1])
    gain_copy = pltpu.make_async_copy(gain_ref, gain, local_h.at[3])
    final_copy = pltpu.make_async_copy(final_ref, final, local_h.at[4])
    gain_copy.start()
    for i, state in enumerate((down_ref, up_ref)):
        pltpu.make_async_copy(
            state.at[0, :, pl.ds(fcol, COLS)], xb.at[i, 0, pl.ds(frow, ROWS), :], local_x.at[i]
        ).start()
    for i in range(2):
        pltpu.make_async_copy(
            value_ref.at[0, i, pl.ds(pl.multiple_of(f * COLS, COLS), COLS), :],
            pw.at[i, :, pl.ds(fhead, 128)], local_w.at[i],
        ).start()

        @pl.when(follows(i)[0])
        def _():
            pltpu.make_async_copy(
                out_ref.at[0, i, :, pl.ds(fcol, COLS)], ow.at[1 - i, pl.ds(fhead, 128), :],
                local_w.at[3 - i],
            ).start()

    barrier = pltpu.get_barrier_semaphore()

    def greet(target):
        pl.semaphore_signal(barrier, inc=1, device_id=target, device_id_type=MESH)

    @pl.loop(1, 16)
    def _(k):
        greet(plane(k)[1])
        greet(pillar(k))

    @pl.when(jnp.logical_not(first))
    def _():
        greet((0, f))

        @pl.loop(0, FS)
        def _(k):
            greet((s - 1, k))

    @pl.when(jnp.logical_not(last))
    def _():
        @pl.loop(0, FS)
        def _(k):
            greet((s + 1, k))

    @pl.when(first)
    def _():
        @pl.loop(1, SEG)
        def _(k):
            greet((k, f))

    pl.semaphore_wait(
        barrier, 30 + jnp.where(first, FS + SEG - 1, 2 * FS + 1) - jnp.where(last, FS, 0)
    )

    def send_states(i, state, lead, section, tick):
        for j in range(1, FS):
            p = lax.rem(f + j, FS)
            put(
                state.at[lead, :, pl.ds(pl.multiple_of(p * COLS, COLS), COLS)],
                xb.at[section, tick, pl.ds(frow, ROWS), :],
                x_s.at[i], x_r.at[i], (s, p),
            )

    def send_value(i, chunk):
        row = pl.multiple_of(chunk * 128, 128)
        for j in range(1, FS):
            p = lax.rem(f + j, FS)
            put(
                value_ref.at[0, i, pl.ds(pl.multiple_of(p * COLS + row, 128), 128), :],
                pw.at[i, pl.ds(row, 128), pl.ds(fhead, 128)], w_s.at[i], w_r.at[i], (s, p),
            )

    def send_out(i, chunk):
        inside, to, slot = follows(i)
        row = pl.multiple_of(chunk * 32, 32)
        for j in range(FS):
            p = lax.rem(f + j, FS)
            send = functools.partial(
                put,
                out_ref.at[0, i, pl.ds(row, 32), pl.ds(pl.multiple_of(p * COLS, COLS), COLS)],
                ow.at[slot, pl.ds(pl.multiple_of(f * 128 + row, 32), 32), :],
                w_s.at[2 + i], w_r.at[2 + slot], (to, p),
            )
            if j == 0:
                pl.when(jnp.logical_not(inside))(send)
            else:
                send()

    def do_send(i, what, chunk):
        pl.when(what == 0)(functools.partial(send_value, i, chunk))
        pl.when(what == 1)(functools.partial(send_out, i, chunk))

    send_states(UP, up_ref, 0, UP, 0)
    send_states(DOWN, down_ref, 0, DOWN, 0)

    @pl.loop(0, 4)
    def _(chunk):
        send_value(UP, chunk)

    head_copy.start()
    teach_copy.start()
    final_copy.start()

    @pl.when(first)
    def _():
        for i in range(2):
            pltpu.make_async_copy(
                new_ref.at[i, :, pl.ds(fcol, COLS)],
                xb.at[DOWN, 1 + i, pl.ds(frow, ROWS), :], local_x.at[2 + i],
            ).start()
            send_states(2 + i, new_ref, i, DOWN, 1 + i)

    gain_copy.wait()

    codes = []
    for i in range(STEPS):
        a, b, d = (step(*rows[i]) for rows in TABLES)
        codes.append(b if a == b == d else jnp.where(first, a, jnp.where(last, d, b)))

    def do_head(section, tick):
        @pl.when(tick == 0)
        def _():
            take(xb.at[section, 0, pl.ds(0, 112), :], x_r.at[section])
            take(xb.at[section, 0, pl.ds(0, ROWS), :], local_x.at[section])
            take(pw.at[section, :, pl.ds(0, 896)], w_r.at[section])
            take(pw.at[section, :, pl.ds(0, 128)], local_w.at[section])

        @pl.when(jnp.logical_and(tick > 0, jnp.logical_and(first, section == DOWN)))
        def _():
            take(xb.at[DOWN, tick, pl.ds(0, 112), :], x_r.at[1 + tick])
            take(xb.at[DOWN, tick, pl.ds(0, ROWS), :], local_x.at[1 + tick])

        rows = xb[section, tick].astype(F32)
        square = jnp.sum(rows * rows, axis=-1, keepdims=True)
        scaled = (rows * gain[0, pl.ds(section, 1), pl.ds(fcol, COLS)]).astype(BF)
        part[section, tick, :, 0:H] = jnp.dot(
            scaled, pw[section], preferred_element_type=F32
        ).astype(BF)
        high = square.astype(BF).astype(F32)
        lane = lax.broadcasted_iota(jnp.int32, (MB, 128), 1)
        part[section, tick, :, H:WIDE] = jnp.where(lane < 64, high, square - high).astype(BF)
        for j in range(1, FS):
            p = lax.rem(f + j, FS)
            put(
                part.at[section, tick, pl.ds(pl.multiple_of(p * ROWS, ROWS), ROWS), :],
                parts.at[section, tick, f], rs_s.at[section, tick], rs_r.at[section, tick], (s, p),
            )
        inside, to, slot = follows(section)

        @pl.when(inside)
        def _():
            xp[1 - section, tick] = xb[section, tick]

        @pl.when(jnp.logical_not(inside))
        def _():
            put(
                xb.at[section, tick], xp.at[section, tick],
                hop_s.at[section, tick], hop_r.at[section, tick], (to, f),
            )

    def do_reduce(section, tick):
        take(parts.at[section, tick, pl.ds(0, FS - 1)], rs_r.at[section, tick])
        total = part[section, tick, pl.ds(frow, ROWS), :].astype(F32)
        for j in range(1, FS):
            total = total + parts[section, tick, lax.rem(f + j, FS)].astype(F32)
        square = total[:, H : H + 1] + total[:, H + 64 : H + 65]
        scale = lax.rsqrt(square * (1.0 / D) + EPS)
        hvo[section, tick] = (total[:, 0:H] * scale).astype(BF)
        inside, to, slot = follows(section)
        for j in range(FS):
            p = lax.rem(f + j, FS)
            send = functools.partial(
                put, hvo.at[section, tick], hv.at[slot, tick, pl.ds(frow, ROWS), :],
                ag_s.at[section, tick], ag_r.at[slot, tick], (to, p),
            )
            if j == 0:
                pl.when(jnp.logical_not(inside))(send)
            else:
                send()

        @pl.when(inside)
        def _():
            hv[1 - section, tick, pl.ds(frow, ROWS), :] = hvo[section, tick]

    def do_out(slot, tick):
        within = jnp.where(slot == DOWN, first, last)

        @pl.when(within)
        def _():
            @pl.when(tick == 0)
            def _():
                take(ow.at[slot, pl.ds(0, 896), :], w_r.at[2 + slot])
                take(ow.at[slot, pl.ds(0, 128), :], local_w.at[2 + slot])

            take(hv.at[slot, tick, pl.ds(0, 112), :], ag_r.at[slot, tick])

        @pl.when(jnp.logical_not(within))
        def _():
            @pl.when(tick == 0)
            def _():
                take(ow.at[slot], w_r.at[2 + slot])

            take(xp.at[slot, tick], hop_r.at[slot, tick])
            take(hv.at[slot, tick], ag_r.at[slot, tick])

        added = jnp.dot(hv[slot, tick], ow[slot], preferred_element_type=F32)
        result = (xp[slot, tick].astype(F32) + added).astype(BF)
        done = jnp.logical_and(first, slot == DOWN)

        @pl.when(jnp.logical_not(done))
        def _():
            xb[slot, tick + 1] = result

        @pl.when(done)
        def _():
            xo[tick] = result
            hid[tick, 0:32, pl.ds(fcol, COLS)] = xo[tick, 0:32, :]

            @pl.loop(1, SEG)
            def _(k):
                to = 1 + lax.rem(k + 14, SEG - 1)
                piece = lax.rem(to, 2) * 2 + lax.rem(lax.div(to, 2), 2)
                row = pl.multiple_of(piece * 32, 32)
                put(
                    xo.at[tick, pl.ds(row, 32), :],
                    hid.at[tick, pl.ds(row, 32), pl.ds(fcol, COLS)],
                    z_s.at[tick, lax.div(to, 4)], z_r.at[tick], (to, f),
                )

    def do_forward(tick):
        mine = hid.at[tick, pl.ds(qrow, 32), pl.ds(fcol, COLS)]

        @pl.when(jnp.logical_not(first))
        def _():
            take(mine, z_r.at[tick])

        @pl.loop(1, 16)
        def _(k):
            x2, target = plane(k)
            other = lax.rem(x + x2, 2)
            put(mine, mine, pl_s.at[tick, other], pl_r.at[tick, other], target)

    def do_share(tick):
        take(hid.at[tick, pl.ds(qrow, 32), pl.ds(0, D - COLS)], pl_r.at[tick, 0])
        take(hid.at[tick, pl.ds(orow, 32), :], pl_r.at[tick, 1])
        half = hid.at[tick, pl.ds(crow, 64), :]
        put(half, half, d2_s.at[tick], d2_r.at[tick], (s + 1 - 2 * c, f))

    def do_logits(tick):
        @pl.when(tick == 0)
        def _():
            head_copy.wait()
            teach_copy.wait()
            final_copy.wait()

        take(hid.at[tick, pl.ds(prow, 64), :], d2_r.at[tick])

        @pl.loop(0, MB // 16)
        def _(i):
            row = pl.multiple_of(i * 16, 16)
            rows = hid[tick, pl.ds(row, 16), :].astype(F32)
            scale = lax.rsqrt(jnp.mean(rows * rows, axis=-1, keepdims=True) + EPS)
            hn[pl.ds(row, 16), :] = (rows * scale * final[...]).astype(BF)

        acc[...] = jnp.zeros_like(acc)

        @pl.loop(0, 4)
        def _(k):
            deep = pl.multiple_of(k * 1024, 1024)
            acc[...] += jnp.dot(
                hn[:, pl.ds(deep, 1024)], head[pl.ds(deep, 1024), :], preferred_element_type=F32
            )

        @pl.loop(0, 4)
        def _(i):
            row = pl.multiple_of(i * 32, 32)
            there = pl.multiple_of(tick * MB + i * 32, 32)
            logits = acc[pl.ds(row, 32), :]
            logit_out[pl.ds(there, 32), :] = logits.astype(BF)
            taught = teach[pl.ds(there, 32), :].astype(F32)
            teach_max = jnp.max(taught, axis=-1, keepdims=True)
            weight = jnp.exp(taught - teach_max)
            teach_sum = jnp.sum(weight, axis=-1, keepdims=True)
            cross = jnp.sum(weight * (taught - logits), axis=-1, keepdims=True)
            stud_max = jnp.max(logits, axis=-1, keepdims=True)
            stud_sum = jnp.sum(jnp.exp(logits - stud_max), axis=-1, keepdims=True)
            lane = lax.broadcasted_iota(jnp.int32, (32, 128), 1)
            packed = jnp.where(lane == 0, teach_max, stud_max)
            packed = jnp.where(lane == 1, teach_sum, packed)
            packed = jnp.where(lane == 2, cross, packed)
            packed = jnp.where(lane == 4, stud_sum, packed)
            cols[pl.ds(row, 32), :] = packed

        slot = x * 4 + y
        st1[tick, slot] = cols[...].T[0:8, :]
        mine = st1.at[tick, slot]

        @pl.loop(1, 16)
        def _(k):
            put(mine, mine, s1_s.at[tick], s1_r.at[tick], plane(k)[1])

    def merged(ref, tick):
        stats = ref[tick]
        teach_max = stats[:, 0, :]
        stud_max = stats[:, 3, :]
        top_teach = jnp.max(teach_max, axis=0, keepdims=True)
        top_stud = jnp.max(stud_max, axis=0, keepdims=True)
        teach_scale = jnp.exp(teach_max - top_teach)
        teach_sum = jnp.sum(stats[:, 1, :] * teach_scale, axis=0, keepdims=True)
        cross = jnp.sum(stats[:, 2, :] * teach_scale, axis=0, keepdims=True)
        stud_sum = jnp.sum(stats[:, 4, :] * jnp.exp(stud_max - top_stud), axis=0, keepdims=True)
        return top_teach, teach_sum, cross, top_stud, stud_sum

    def do_merge(tick):
        take(st1.at[tick, pl.ds(0, 15)], s1_r.at[tick])
        slot = z * 2 + c
        for i, row in enumerate(merged(st1, tick)):
            st2[tick, slot, i : i + 1, :] = row
        for i in range(5, 8):
            st2[tick, slot, i : i + 1, :] = jnp.zeros((1, 128), F32)
        mine = st2.at[tick, slot]

        @pl.loop(1, 16)
        def _(k):
            put(mine, mine, s2_s.at[tick], s2_r.at[tick], pillar(k))

    def do_finish(tick):
        take(st2.at[tick, pl.ds(0, 15)], s2_r.at[tick])
        teach_max, teach_sum, cross, stud_max, stud_sum = merged(st2, tick)
        div_out[pl.ds(tick, 1), :] = (
            cross / teach_sum - teach_max - jnp.log(teach_sum) + stud_max + jnp.log(stud_sum)
        )

    def do_spread(section):
        fresh = jnp.logical_and(first, section == DOWN)

        @pl.when(jnp.logical_not(fresh))
        def _():
            fin[section, :, pl.ds(fcol, COLS)] = xb[section, TICKS, pl.ds(frow, ROWS), :]
            for j in range(1, FS):
                p = lax.rem(f + j, FS)
                put(
                    xb.at[section, TICKS, pl.ds(pl.multiple_of(p * ROWS, ROWS), ROWS), :],
                    fin.at[section, :, pl.ds(fcol, COLS)], f_s.at[section], f_r.at[section], (s, p),
                )

        @pl.when(fresh)
        def _():
            fresh_copy = pltpu.make_async_copy(new_ref.at[TICKS - 1], fin.at[DOWN], local_h.at[2])
            fresh_copy.start()
            fresh_copy.wait()

    @pl.loop(0, STEPS)
    def _(i):
        code = jnp.int32(0)
        for k in range(STEPS):
            code = jnp.where(i == k, codes[k], code)
        kind = lax.div(code, 8)
        section = lax.rem(lax.div(code, 4), 2)
        tick = lax.rem(code, 4)

        pl.when(kind == SEND_DOWN)(functools.partial(do_send, DOWN, section, tick))
        pl.when(kind == SEND_UP)(functools.partial(do_send, UP, section, tick))
        pl.when(kind == HEAD)(functools.partial(do_head, section, tick))
        pl.when(kind == REDUCE)(functools.partial(do_reduce, section, tick))
        pl.when(kind == OUT)(functools.partial(do_out, section, tick))
        pl.when(kind == FORWARD)(functools.partial(do_forward, tick))
        pl.when(kind == SHARE)(functools.partial(do_share, tick))
        pl.when(kind == LOGITS)(functools.partial(do_logits, tick))
        pl.when(kind == MERGE)(functools.partial(do_merge, tick))
        pl.when(kind == FINISH)(functools.partial(do_finish, tick))
        pl.when(kind == SPREAD)(functools.partial(do_spread, section))

    @pl.when(jnp.logical_not(first))
    def _():
        take(fin.at[DOWN, :, pl.ds(0, D - COLS)], f_r.at[DOWN])
        take(fin.at[DOWN, :, pl.ds(0, D - COLS)], f_s.at[DOWN])

    take(fin.at[UP, :, pl.ds(0, D - COLS)], f_r.at[UP])
    take(fin.at[UP, :, pl.ds(0, D - COLS)], f_s.at[UP])
    down_out[0] = fin[DOWN]
    up_out[0] = fin[UP]

    @pl.loop(0, 2)
    def _(i):
        take(pw.at[i, :, pl.ds(0, 896)], w_s.at[i])

        @pl.when(follows(i)[0])
        def _():
            take(ow.at[i, pl.ds(0, 896), :], w_s.at[2 + i])

        @pl.when(jnp.logical_not(follows(i)[0]))
        def _():
            take(ow.at[i], w_s.at[2 + i])

        take(xb.at[i, 0, pl.ds(0, 112), :], x_s.at[i])

    @pl.when(first)
    def _():
        @pl.loop(2, 4)
        def _(i):
            take(xb.at[DOWN, 0, pl.ds(0, 112), :], x_s.at[i])

    @pl.loop(0, TICKS)
    def _(tick):
        for section in range(2):
            take(parts.at[section, tick, pl.ds(0, FS - 1)], rs_s.at[section, tick])
            inside = follows(section)[0]

            @pl.when(inside)
            def _():
                take(hv.at[section, tick, pl.ds(0, 112), :], ag_s.at[section, tick])

            @pl.when(jnp.logical_not(inside))
            def _():
                take(hv.at[section, tick], ag_s.at[section, tick])
                take(xp.at[section, tick], hop_s.at[section, tick])

        @pl.when(first)
        def _():
            take(xo.at[tick, pl.ds(0, 96), :], z_s.at[tick, 0])

            @pl.loop(1, 8)
            def _(k):
                take(xo.at[tick], z_s.at[tick, k])

        take(hid.at[tick, pl.ds(qrow, 32), pl.ds(0, D - COLS)], pl_s.at[tick, 0])
        take(hid.at[tick, pl.ds(orow, 32), :], pl_s.at[tick, 1])
        take(hid.at[tick, pl.ds(crow, 64), :], d2_s.at[tick])
        take(st1.at[tick, pl.ds(0, 15)], s1_s.at[tick])
        take(st2.at[tick, pl.ds(0, 15)], s2_s.at[tick])


def hand_over(*refs):
    count = len(refs) // 2
    for i in range(count):
        refs[count + i][...] = refs[i][...]


def local(
    new_batches, down_state, up_state, gains, w_value, w_out, final_gain, lm_head, teacher_logits
):
    hbm = pl.BlockSpec(memory_space=pl.ANY)
    vmem = pl.BlockSpec(memory_space=pltpu.VMEM)
    dma = pltpu.SemaphoreType.DMA
    down, up, logits, divergence = pl.pallas_call(
        kernel,
        out_shape=(
            jax.ShapeDtypeStruct((1, ROWS, D), BF),
            jax.ShapeDtypeStruct((1, ROWS, D), BF),
            jax.ShapeDtypeStruct((TICKS * MB, VOC), BF),
            jax.ShapeDtypeStruct((TICKS, MB), F32),
        ),
        in_specs=[hbm, hbm, hbm, hbm, hbm, hbm, hbm, hbm, hbm],
        out_specs=(vmem, vmem, vmem, vmem),
        scratch_shapes=[
            pltpu.VMEM((2, COLS, H), BF),
            pltpu.VMEM((2, H, COLS), BF),
            pltpu.VMEM((2, TICKS + 1, MB, COLS), BF),
            pltpu.VMEM((2, TICKS, MB, COLS), BF),
            pltpu.VMEM((2, TICKS, MB, WIDE), BF),
            pltpu.VMEM((2, TICKS, FS, ROWS, WIDE), BF),
            pltpu.VMEM((2, TICKS, ROWS, H), BF),
            pltpu.VMEM((2, TICKS, MB, H), BF),
            pltpu.VMEM((TICKS, MB, COLS), BF),
            pltpu.VMEM((TICKS, MB, D), BF),
            pltpu.VMEM((MB, D), BF),
            pltpu.VMEM((MB, VOC), F32),
            pltpu.VMEM((D, VOC), BF),
            pltpu.VMEM((TICKS * MB, VOC), BF),
            pltpu.VMEM((MB, 128), F32),
            pltpu.VMEM((TICKS, 16, 8, 128), F32),
            pltpu.VMEM((TICKS, 16, 8, 128), F32),
            pltpu.VMEM((2, ROWS, D), BF),
            pltpu.VMEM((1, 2, D), F32),
            pltpu.VMEM((1, D), F32),
            dma((4,)), dma((4,)), dma((5,)),
            dma((4,)), dma((4,)), dma((4,)), dma((4,)),
            dma((2, TICKS)), dma((2, TICKS)), dma((2, TICKS)), dma((2, TICKS)),
            dma((2, TICKS)), dma((2, TICKS)),
            dma((TICKS, 8)), dma((TICKS,)),
            dma((TICKS, 2)), dma((TICKS, 2)),
            dma((TICKS,)), dma((TICKS,)),
            dma((TICKS,)), dma((TICKS,)), dma((TICKS,)), dma((TICKS,)),
            dma((2,)), dma((2,)),
        ],
        compiler_params=pltpu.CompilerParams(
            collective_id=0, has_side_effects=True, vmem_limit_bytes=VMEM_LIMIT
        ),
        name="ticks_and_loss",
    )(
        new_batches, down_state, up_state, gains, w_value, w_out,
        final_gain.reshape(1, D), lm_head, teacher_logits,
    )
    whole = (down, up, logits, divergence)
    down, up, logits, divergence = pl.pallas_call(
        hand_over,
        out_shape=tuple(jax.ShapeDtypeStruct(one.shape, one.dtype) for one in whole),
        in_specs=[vmem] * 4,
        out_specs=(vmem,) * 4,
        compiler_params=pltpu.CompilerParams(vmem_limit_bytes=VMEM_LIMIT),
        name="hand_over",
    )(*whole)
    return (down, up, logits, divergence.reshape(TICKS * MB))


def solution(mesh):
    placed = (
        P(None, "fsdp", None),
        P("segment", "fsdp", None),
        P("segment", "fsdp", None),
        P("segment", None, None),
        P("segment", None, None, "fsdp"),
        P("segment", None, "fsdp", None),
        P(),
        P(None, ("segment", "fsdp")),
        P(None, ("segment", "fsdp")),
    )
    return jax.shard_map(
        local,
        mesh=mesh,
        in_specs=placed,
        out_specs=(
            P("segment", "fsdp", None),
            P("segment", "fsdp", None),
            P(None, ("segment", "fsdp")),
            P(),
        ),
        check_vma=False,
    )
```

```python
import functools

import jax
import jax.numpy as jnp
from jax import lax
from jax.experimental import pallas as pl
from jax.experimental.pallas import tpu as pltpu
from jax.sharding import PartitionSpec as P

MESH = pl.DeviceIdType.MESH
BF = jnp.bfloat16
F32 = jnp.float32
EPS = 1e-06

D = 4096
H = 1024
FS = 8
SEG = 32
MB = 128
TICKS = 3
ROWS = MB // FS
COLS = D // FS
WIDE = H + 128
VOC = 512
DOWN, UP = 0, 1
VMEM_LIMIT = 64 * 1024 * 1024 - 65536

(SEND_DOWN, SEND_UP, HEAD, REDUCE, OUT, FORWARD, SHARE, LOGITS, MERGE, FINISH, SPREAD, NOTHING) = range(12)


def step(kind, section=0, tick=0):
    return kind * 8 + section * 4 + tick


def parse(words):
    names = {
        "W": SEND_DOWN, "V": SEND_UP, "A": HEAD, "B": REDUCE, "C": OUT, "D": FORWARD, "E": SHARE,
        "F": LOGITS, "G": MERGE, "H": FINISH, "I": SPREAD,
    }
    steps = []
    for word in words:
        section, tick = 0, 0
        for mark in word[1:]:
            if mark in "du":
                section = "du".index(mark)
            else:
                tick = int(mark)
        steps.append((names[word[0]], section, tick))
    return steps


FIRST = (
    "Vu0", "Au0", "Vu1", "Vu2", "Vu3", "Wd0", "Bu0", "Wd1", "Cd0", "D0", "Cu0", "Au1",
    "Wd2", "Wd3", "Bu1", "Wu0", "Cd1", "D1", "Cu1", "Au2", "Wu1", "Wu2", "Bu2", "Wu3",
    "Ad0", "Cd2", "D2", "Ad1", "E0", "Bd0", "Bd1", "F0", "Ad2", "E1", "Bd2", "F1",
    "Cu2", "Iu", "Id", "E2", "F2", "G0", "G1", "G2", "H0", "H1", "H2",
)
MIDDLE = (
    "Vu0", "Au0", "Vu1", "Vu2", "Vu3", "Wd0", "Bu0", "Wd1", "Cu0", "Au1", "Wd2", "Wd3",
    "Bu1", "Wu0", "Wu1", "Wu2", "Wu3", "D0", "Ad0", "E0", "Bd0", "D1", "Cd0", "Ad1",
    "Cu1", "Au2", "E1", "F0", "Bd1", "Bu2", "D2", "Cd1", "Ad2", "Cu2", "E2", "F1",
    "Bd2", "F2", "Cd2", "Iu", "Id", "G0", "G1", "G2", "H0", "H1", "H2",
)
LAST = (
    "Vu0", "Au0", "Vu1", "Vu2", "Vu3", "Wd0", "Bu0", "Wd1", "Wd2", "Wd3", "Wu0", "Wu1",
    "Wu2", "Wu3", "D0", "Ad0", "E0", "Bd0", "Cu0", "Au1", "D1", "Cd0", "Ad1", "Bu1",
    "E1", "Bd1", "Cu1", "Au2", "F0", "Cd1", "Ad2", "Bu2", "Bd2", "D2", "F1", "Cu2",
    "Iu", "E2", "Cd2", "Id", "F2", "G0", "G1", "G2", "H0", "H1", "H2",
)
TABLES = [parse(FIRST), parse(MIDDLE), parse(LAST)]
STEPS = max(len(table) for table in TABLES)
TABLES = [table + [(NOTHING, 0, 0)] * (STEPS - len(table)) for table in TABLES]


def take(ref, sem):
    pltpu.make_async_copy(ref, ref, sem).wait()


def kernel(
    new_ref, down_ref, up_ref, gain_ref, value_ref, out_ref, final_ref, head_ref, teach_ref,
    down_out, up_out, logit_out, div_out,
    pw, ow, xb, xp, part, parts, hvo, hv, xo, hid, hn, acc, head, teach, heavy, known, cols, st1, st2, fin,
    gain, final, local_w, local_x, local_h,
    w_s, w_r, x_s, x_r, rs_s, rs_r, ag_s, ag_r, hop_s, hop_r, z_s, z_r, pl_s, pl_r, d2_s, d2_r,
    s1_s, s1_r, s2_s, s2_r, f_s, f_r,
):
    s = lax.axis_index("segment")
    f = lax.axis_index("fsdp")
    z, xl, c = lax.div(s, 4), lax.rem(lax.div(s, 2), 2), lax.rem(s, 2)
    y, xh = lax.div(f, 2), lax.rem(f, 2)
    x = xh * 2 + xl
    first, last = s == 0, s == SEG - 1
    frow = pl.multiple_of(f * ROWS, ROWS)
    fcol = pl.multiple_of(f * COLS, COLS)
    fhead = pl.multiple_of(f * 128, 128)
    quarter = c * 2 + xl
    qrow = pl.multiple_of(quarter * 32, 32)
    orow = pl.multiple_of((c * 2 + 1 - xl) * 32, 32)
    crow = pl.multiple_of(c * 64, 64)
    prow = pl.multiple_of((1 - c) * 64, 64)

    def follows(section):
        inside = jnp.where(section == DOWN, last, first)
        ahead = jnp.where(section == DOWN, 1, -1)
        return inside, s + jnp.where(inside, 0, ahead), jnp.where(inside, 1 - section, section)

    def plane(k):
        x2, y2 = lax.rem(x + lax.rem(k, 4), 4), lax.rem(y + lax.div(k, 4), 4)
        return x2, (z * 4 + lax.rem(x2, 2) * 2 + c, y2 * 2 + lax.div(x2, 2))

    def pillar(k):
        z2, c2 = lax.rem(z + lax.div(k, 2), 8), lax.rem(c + lax.rem(k, 2), 2)
        return (z2 * 4 + xl * 2 + c2, f)

    def put(src, dst, send, recv, target):
        pltpu.make_async_remote_copy(
            src_ref=src, dst_ref=dst, send_sem=send, recv_sem=recv,
            device_id=target, device_id_type=MESH,
        ).start()

    head_copy = pltpu.make_async_copy(head_ref, head, local_h.at[0])
    teach_copy = pltpu.make_async_copy(teach_ref, teach, local_h.at[1])
    gain_copy = pltpu.make_async_copy(gain_ref, gain, local_h.at[3])
    final_copy = pltpu.make_async_copy(final_ref, final, local_h.at[4])
    gain_copy.start()
    for i, state in enumerate((down_ref, up_ref)):
        pltpu.make_async_copy(
            state.at[0, :, pl.ds(fcol, COLS)], xb.at[i, 0, pl.ds(frow, ROWS), :], local_x.at[i]
        ).start()
    for i in range(2):
        pltpu.make_async_copy(
            value_ref.at[0, i, pl.ds(pl.multiple_of(f * COLS, COLS), COLS), :],
            pw.at[i, :, pl.ds(fhead, 128)], local_w.at[i],
        ).start()

        @pl.when(follows(i)[0])
        def _():
            pltpu.make_async_copy(
                out_ref.at[0, i, :, pl.ds(fcol, COLS)], ow.at[1 - i, pl.ds(fhead, 128), :],
                local_w.at[3 - i],
            ).start()

    barrier = pltpu.get_barrier_semaphore()

    def greet(target):
        pl.semaphore_signal(barrier, inc=1, device_id=target, device_id_type=MESH)

    @pl.loop(1, 16)
    def _(k):
        greet(plane(k)[1])
        greet(pillar(k))

    @pl.when(jnp.logical_not(first))
    def _():
        greet((0, f))

        @pl.loop(0, FS)
        def _(k):
            greet((s - 1, k))

    @pl.when(jnp.logical_not(last))
    def _():
        @pl.loop(0, FS)
        def _(k):
            greet((s + 1, k))

    @pl.when(first)
    def _():
        @pl.loop(1, SEG)
        def _(k):
            greet((k, f))

    pl.semaphore_wait(
        barrier, 30 + jnp.where(first, FS + SEG - 1, 2 * FS + 1) - jnp.where(last, FS, 0)
    )

    def send_states(i, state, lead, section, tick):
        for j in range(1, FS):
            p = lax.rem(f + j, FS)
            put(
                state.at[lead, :, pl.ds(pl.multiple_of(p * COLS, COLS), COLS)],
                xb.at[section, tick, pl.ds(frow, ROWS), :],
                x_s.at[i], x_r.at[i], (s, p),
            )

    def send_value(i, chunk):
        row = pl.multiple_of(chunk * 128, 128)
        for j in range(1, FS):
            p = lax.rem(f + j, FS)
            put(
                value_ref.at[0, i, pl.ds(pl.multiple_of(p * COLS + row, 128), 128), :],
                pw.at[i, pl.ds(row, 128), pl.ds(fhead, 128)], w_s.at[i], w_r.at[i], (s, p),
            )

    def send_out(i, chunk):
        inside, to, slot = follows(i)
        row = pl.multiple_of(chunk * 32, 32)
        for j in range(FS):
            p = lax.rem(f + j, FS)
            send = functools.partial(
                put,
                out_ref.at[0, i, pl.ds(row, 32), pl.ds(pl.multiple_of(p * COLS, COLS), COLS)],
                ow.at[slot, pl.ds(pl.multiple_of(f * 128 + row, 32), 32), :],
                w_s.at[2 + i], w_r.at[2 + slot], (to, p),
            )
            if j == 0:
                pl.when(jnp.logical_not(inside))(send)
            else:
                send()

    def do_send(i, what, chunk):
        pl.when(what == 0)(functools.partial(send_value, i, chunk))
        pl.when(what == 1)(functools.partial(send_out, i, chunk))

    send_states(UP, up_ref, 0, UP, 0)
    send_states(DOWN, down_ref, 0, DOWN, 0)

    @pl.loop(0, 4)
    def _(chunk):
        send_value(UP, chunk)

    head_copy.start()
    teach_copy.start()
    final_copy.start()

    @pl.when(first)
    def _():
        for i in range(2):
            pltpu.make_async_copy(
                new_ref.at[i, :, pl.ds(fcol, COLS)],
                xb.at[DOWN, 1 + i, pl.ds(frow, ROWS), :], local_x.at[2 + i],
            ).start()
            send_states(2 + i, new_ref, i, DOWN, 1 + i)

    gain_copy.wait()
    teach_copy.wait()

    @pl.loop(0, TICKS * MB // 32)
    def _(i):
        row = pl.multiple_of(i * 32, 32)
        taught = teach[pl.ds(row, 32), :].astype(F32)
        teach_max = jnp.max(taught, axis=-1, keepdims=True)
        weight = jnp.exp(taught - teach_max)
        heavy[pl.ds(row, 32), :] = weight
        lane = lax.broadcasted_iota(jnp.int32, (32, 128), 1)
        known[pl.ds(row, 32), :] = jnp.where(
            lane == 0, teach_max, jnp.sum(weight, axis=-1, keepdims=True)
        )


    codes = []
    for i in range(STEPS):
        a, b, d = (step(*rows[i]) for rows in TABLES)
        codes.append(b if a == b == d else jnp.where(first, a, jnp.where(last, d, b)))

    def do_head(section, tick):
        @pl.when(tick == 0)
        def _():
            take(xb.at[section, 0, pl.ds(0, 112), :], x_r.at[section])
            take(xb.at[section, 0, pl.ds(0, ROWS), :], local_x.at[section])
            take(pw.at[section, :, pl.ds(0, 896)], w_r.at[section])
            take(pw.at[section, :, pl.ds(0, 128)], local_w.at[section])

        @pl.when(jnp.logical_and(tick > 0, jnp.logical_and(first, section == DOWN)))
        def _():
            take(xb.at[DOWN, tick, pl.ds(0, 112), :], x_r.at[1 + tick])
            take(xb.at[DOWN, tick, pl.ds(0, ROWS), :], local_x.at[1 + tick])

        rows = xb[section, tick].astype(F32)
        square = jnp.sum(rows * rows, axis=-1, keepdims=True)
        scaled = (rows * gain[0, pl.ds(section, 1), pl.ds(fcol, COLS)]).astype(BF)
        part[section, tick, :, 0:H] = jnp.dot(
            scaled, pw[section], preferred_element_type=F32
        ).astype(BF)
        high = square.astype(BF).astype(F32)
        lane = lax.broadcasted_iota(jnp.int32, (MB, 128), 1)
        part[section, tick, :, H:WIDE] = jnp.where(lane < 64, high, square - high).astype(BF)
        for j in range(1, FS):
            p = lax.rem(f + j, FS)
            put(
                part.at[section, tick, pl.ds(pl.multiple_of(p * ROWS, ROWS), ROWS), :],
                parts.at[section, tick, f], rs_s.at[section, tick], rs_r.at[section, tick], (s, p),
            )
        inside, to, slot = follows(section)

        @pl.when(inside)
        def _():
            xp[1 - section, tick] = xb[section, tick]

        @pl.when(jnp.logical_not(inside))
        def _():
            put(
                xb.at[section, tick], xp.at[section, tick],
                hop_s.at[section, tick], hop_r.at[section, tick], (to, f),
            )

    def do_reduce(section, tick):
        take(parts.at[section, tick, pl.ds(0, FS - 1)], rs_r.at[section, tick])
        total = part[section, tick, pl.ds(frow, ROWS), :].astype(F32)
        for j in range(1, FS):
            total = total + parts[section, tick, lax.rem(f + j, FS)].astype(F32)
        square = total[:, H : H + 1] + total[:, H + 64 : H + 65]
        scale = lax.rsqrt(square * (1.0 / D) + EPS)
        hvo[section, tick] = (total[:, 0:H] * scale).astype(BF)
        inside, to, slot = follows(section)
        for j in range(FS):
            p = lax.rem(f + j, FS)
            send = functools.partial(
                put, hvo.at[section, tick], hv.at[slot, tick, pl.ds(frow, ROWS), :],
                ag_s.at[section, tick], ag_r.at[slot, tick], (to, p),
            )
            if j == 0:
                pl.when(jnp.logical_not(inside))(send)
            else:
                send()

        @pl.when(inside)
        def _():
            hv[1 - section, tick, pl.ds(frow, ROWS), :] = hvo[section, tick]

    def do_out(slot, tick):
        within = jnp.where(slot == DOWN, first, last)

        @pl.when(within)
        def _():
            @pl.when(tick == 0)
            def _():
                take(ow.at[slot, pl.ds(0, 896), :], w_r.at[2 + slot])
                take(ow.at[slot, pl.ds(0, 128), :], local_w.at[2 + slot])

            take(hv.at[slot, tick, pl.ds(0, 112), :], ag_r.at[slot, tick])

        @pl.when(jnp.logical_not(within))
        def _():
            @pl.when(tick == 0)
            def _():
                take(ow.at[slot], w_r.at[2 + slot])

            take(xp.at[slot, tick], hop_r.at[slot, tick])
            take(hv.at[slot, tick], ag_r.at[slot, tick])

        added = jnp.dot(hv[slot, tick], ow[slot], preferred_element_type=F32)
        result = (xp[slot, tick].astype(F32) + added).astype(BF)
        done = jnp.logical_and(first, slot == DOWN)

        @pl.when(jnp.logical_not(done))
        def _():
            xb[slot, tick + 1] = result

        @pl.when(done)
        def _():
            xo[tick] = result
            hid[tick, 0:32, pl.ds(fcol, COLS)] = xo[tick, 0:32, :]

            @pl.loop(1, SEG)
            def _(k):
                to = 1 + lax.rem(k + 14, SEG - 1)
                piece = lax.rem(to, 2) * 2 + lax.rem(lax.div(to, 2), 2)
                row = pl.multiple_of(piece * 32, 32)
                put(
                    xo.at[tick, pl.ds(row, 32), :],
                    hid.at[tick, pl.ds(row, 32), pl.ds(fcol, COLS)],
                    z_s.at[tick, lax.div(to, 4)], z_r.at[tick], (to, f),
                )

    def do_forward(tick):
        mine = hid.at[tick, pl.ds(qrow, 32), pl.ds(fcol, COLS)]

        @pl.when(jnp.logical_not(first))
        def _():
            take(mine, z_r.at[tick])

        @pl.loop(1, 16)
        def _(k):
            x2, target = plane(k)
            other = lax.rem(x + x2, 2)
            put(mine, mine, pl_s.at[tick, other], pl_r.at[tick, other], target)

    def do_share(tick):
        take(hid.at[tick, pl.ds(qrow, 32), pl.ds(0, D - COLS)], pl_r.at[tick, 0])
        take(hid.at[tick, pl.ds(orow, 32), :], pl_r.at[tick, 1])
        half = hid.at[tick, pl.ds(crow, 64), :]
        put(half, half, d2_s.at[tick], d2_r.at[tick], (s + 1 - 2 * c, f))

    def do_logits(tick):
        @pl.when(tick == 0)
        def _():
            head_copy.wait()
            final_copy.wait()

        take(hid.at[tick, pl.ds(prow, 64), :], d2_r.at[tick])

        @pl.loop(0, MB // 16)
        def _(i):
            row = pl.multiple_of(i * 16, 16)
            rows = hid[tick, pl.ds(row, 16), :].astype(F32)
            scale = lax.rsqrt(jnp.mean(rows * rows, axis=-1, keepdims=True) + EPS)
            hn[pl.ds(row, 16), :] = (rows * scale * final[...]).astype(BF)

        acc[...] = jnp.dot(hn[...], head[...], preferred_element_type=F32)

        @pl.loop(0, 4)
        def _(i):
            row = pl.multiple_of(i * 32, 32)
            there = pl.multiple_of(tick * MB + i * 32, 32)
            logits = acc[pl.ds(row, 32), :]
            logit_out[pl.ds(there, 32), :] = logits.astype(BF)
            taught = teach[pl.ds(there, 32), :].astype(F32)
            cross = jnp.sum(heavy[pl.ds(there, 32), :] * (taught - logits), axis=-1, keepdims=True)
            stud_max = jnp.max(logits, axis=-1, keepdims=True)
            stud_sum = jnp.sum(jnp.exp(logits - stud_max), axis=-1, keepdims=True)
            lane = lax.broadcasted_iota(jnp.int32, (32, 128), 1)
            packed = jnp.where(lane < 2, known[pl.ds(there, 32), :], stud_max)
            packed = jnp.where(lane == 2, cross, packed)
            packed = jnp.where(lane == 4, stud_sum, packed)
            cols[pl.ds(row, 32), :] = packed

        slot = x * 4 + y
        st1[tick, slot] = cols[...].T[0:8, :]
        mine = st1.at[tick, slot]

        @pl.loop(1, 16)
        def _(k):
            put(mine, mine, s1_s.at[tick], s1_r.at[tick], plane(k)[1])

    def merged(ref, tick):
        stats = ref[tick]
        teach_max = stats[:, 0, :]
        stud_max = stats[:, 3, :]
        top_teach = jnp.max(teach_max, axis=0, keepdims=True)
        top_stud = jnp.max(stud_max, axis=0, keepdims=True)
        teach_scale = jnp.exp(teach_max - top_teach)
        teach_sum = jnp.sum(stats[:, 1, :] * teach_scale, axis=0, keepdims=True)
        cross = jnp.sum(stats[:, 2, :] * teach_scale, axis=0, keepdims=True)
        stud_sum = jnp.sum(stats[:, 4, :] * jnp.exp(stud_max - top_stud), axis=0, keepdims=True)
        return top_teach, teach_sum, cross, top_stud, stud_sum

    def do_merge(tick):
        take(st1.at[tick, pl.ds(0, 15)], s1_r.at[tick])
        slot = z * 2 + c
        for i, row in enumerate(merged(st1, tick)):
            st2[tick, slot, i : i + 1, :] = row
        for i in range(5, 8):
            st2[tick, slot, i : i + 1, :] = jnp.zeros((1, 128), F32)
        mine = st2.at[tick, slot]

        @pl.loop(1, 16)
        def _(k):
            put(mine, mine, s2_s.at[tick], s2_r.at[tick], pillar(k))

    def do_finish(tick):
        take(st2.at[tick, pl.ds(0, 15)], s2_r.at[tick])
        teach_max, teach_sum, cross, stud_max, stud_sum = merged(st2, tick)
        div_out[pl.ds(tick, 1), :] = (
            cross / teach_sum - teach_max - jnp.log(teach_sum) + stud_max + jnp.log(stud_sum)
        )

    def do_spread(section):
        fresh = jnp.logical_and(first, section == DOWN)

        @pl.when(jnp.logical_not(fresh))
        def _():
            fin[section, :, pl.ds(fcol, COLS)] = xb[section, TICKS, pl.ds(frow, ROWS), :]
            for j in range(1, FS):
                p = lax.rem(f + j, FS)
                put(
                    xb.at[section, TICKS, pl.ds(pl.multiple_of(p * ROWS, ROWS), ROWS), :],
                    fin.at[section, :, pl.ds(fcol, COLS)], f_s.at[section], f_r.at[section], (s, p),
                )

        @pl.when(fresh)
        def _():
            fresh_copy = pltpu.make_async_copy(new_ref.at[TICKS - 1], fin.at[DOWN], local_h.at[2])
            fresh_copy.start()
            fresh_copy.wait()

    @pl.loop(0, STEPS)
    def _(i):
        code = jnp.int32(0)
        for k in range(STEPS):
            code = jnp.where(i == k, codes[k], code)
        kind = lax.div(code, 8)
        section = lax.rem(lax.div(code, 4), 2)
        tick = lax.rem(code, 4)

        pl.when(kind == SEND_DOWN)(functools.partial(do_send, DOWN, section, tick))
        pl.when(kind == SEND_UP)(functools.partial(do_send, UP, section, tick))
        pl.when(kind == HEAD)(functools.partial(do_head, section, tick))
        pl.when(kind == REDUCE)(functools.partial(do_reduce, section, tick))
        pl.when(kind == OUT)(functools.partial(do_out, section, tick))
        pl.when(kind == FORWARD)(functools.partial(do_forward, tick))
        pl.when(kind == SHARE)(functools.partial(do_share, tick))
        pl.when(kind == LOGITS)(functools.partial(do_logits, tick))
        pl.when(kind == MERGE)(functools.partial(do_merge, tick))
        pl.when(kind == FINISH)(functools.partial(do_finish, tick))
        pl.when(kind == SPREAD)(functools.partial(do_spread, section))

    @pl.when(jnp.logical_not(first))
    def _():
        take(fin.at[DOWN, :, pl.ds(0, D - COLS)], f_r.at[DOWN])
        take(fin.at[DOWN, :, pl.ds(0, D - COLS)], f_s.at[DOWN])

    take(fin.at[UP, :, pl.ds(0, D - COLS)], f_r.at[UP])
    take(fin.at[UP, :, pl.ds(0, D - COLS)], f_s.at[UP])
    down_out[0] = fin[DOWN]
    up_out[0] = fin[UP]

    @pl.loop(0, 2)
    def _(i):
        take(pw.at[i, :, pl.ds(0, 896)], w_s.at[i])

        @pl.when(follows(i)[0])
        def _():
            take(ow.at[i, pl.ds(0, 896), :], w_s.at[2 + i])

        @pl.when(jnp.logical_not(follows(i)[0]))
        def _():
            take(ow.at[i], w_s.at[2 + i])

        take(xb.at[i, 0, pl.ds(0, 112), :], x_s.at[i])

    @pl.when(first)
    def _():
        @pl.loop(2, 4)
        def _(i):
            take(xb.at[DOWN, 0, pl.ds(0, 112), :], x_s.at[i])

    @pl.loop(0, TICKS)
    def _(tick):
        for section in range(2):
            take(parts.at[section, tick, pl.ds(0, FS - 1)], rs_s.at[section, tick])
            inside = follows(section)[0]

            @pl.when(inside)
            def _():
                take(hv.at[section, tick, pl.ds(0, 112), :], ag_s.at[section, tick])

            @pl.when(jnp.logical_not(inside))
            def _():
                take(hv.at[section, tick], ag_s.at[section, tick])
                take(xp.at[section, tick], hop_s.at[section, tick])

        @pl.when(first)
        def _():
            take(xo.at[tick, pl.ds(0, 96), :], z_s.at[tick, 0])

            @pl.loop(1, 8)
            def _(k):
                take(xo.at[tick], z_s.at[tick, k])

        take(hid.at[tick, pl.ds(qrow, 32), pl.ds(0, D - COLS)], pl_s.at[tick, 0])
        take(hid.at[tick, pl.ds(orow, 32), :], pl_s.at[tick, 1])
        take(hid.at[tick, pl.ds(crow, 64), :], d2_s.at[tick])
        take(st1.at[tick, pl.ds(0, 15)], s1_s.at[tick])
        take(st2.at[tick, pl.ds(0, 15)], s2_s.at[tick])


def hand_over(*refs):
    count = len(refs) // 2
    for i in range(count):
        refs[count + i][...] = refs[i][...]


def local(
    new_batches, down_state, up_state, gains, w_value, w_out, final_gain, lm_head, teacher_logits
):
    hbm = pl.BlockSpec(memory_space=pl.ANY)
    vmem = pl.BlockSpec(memory_space=pltpu.VMEM)
    dma = pltpu.SemaphoreType.DMA
    down, up, logits, divergence = pl.pallas_call(
        kernel,
        out_shape=(
            jax.ShapeDtypeStruct((1, ROWS, D), BF),
            jax.ShapeDtypeStruct((1, ROWS, D), BF),
            jax.ShapeDtypeStruct((TICKS * MB, VOC), BF),
            jax.ShapeDtypeStruct((TICKS, MB), F32),
        ),
        in_specs=[hbm, hbm, hbm, hbm, hbm, hbm, hbm, hbm, hbm],
        out_specs=(vmem, vmem, vmem, vmem),
        scratch_shapes=[
            pltpu.VMEM((2, COLS, H), BF),
            pltpu.VMEM((2, H, COLS), BF),
            pltpu.VMEM((2, TICKS + 1, MB, COLS), BF),
            pltpu.VMEM((2, TICKS, MB, COLS), BF),
            pltpu.VMEM((2, TICKS, MB, WIDE), BF),
            pltpu.VMEM((2, TICKS, FS, ROWS, WIDE), BF),
            pltpu.VMEM((2, TICKS, ROWS, H), BF),
            pltpu.VMEM((2, TICKS, MB, H), BF),
            pltpu.VMEM((TICKS, MB, COLS), BF),
            pltpu.VMEM((TICKS, MB, D), BF),
            pltpu.VMEM((MB, D), BF),
            pltpu.VMEM((MB, VOC), F32),
            pltpu.VMEM((D, VOC), BF),
            pltpu.VMEM((TICKS * MB, VOC), BF),
            pltpu.VMEM((TICKS * MB, VOC), F32),
            pltpu.VMEM((TICKS * MB, 128), F32),
            pltpu.VMEM((MB, 128), F32),
            pltpu.VMEM((TICKS, 16, 8, 128), F32),
            pltpu.VMEM((TICKS, 16, 8, 128), F32),
            pltpu.VMEM((2, ROWS, D), BF),
            pltpu.VMEM((1, 2, D), F32),
            pltpu.VMEM((1, D), F32),
            dma((4,)), dma((4,)), dma((5,)),
            dma((4,)), dma((4,)), dma((4,)), dma((4,)),
            dma((2, TICKS)), dma((2, TICKS)), dma((2, TICKS)), dma((2, TICKS)),
            dma((2, TICKS)), dma((2, TICKS)),
            dma((TICKS, 8)), dma((TICKS,)),
            dma((TICKS, 2)), dma((TICKS, 2)),
            dma((TICKS,)), dma((TICKS,)),
            dma((TICKS,)), dma((TICKS,)), dma((TICKS,)), dma((TICKS,)),
            dma((2,)), dma((2,)),
        ],
        compiler_params=pltpu.CompilerParams(
            collective_id=0, has_side_effects=True, vmem_limit_bytes=VMEM_LIMIT
        ),
        name="ticks_and_loss",
    )(
        new_batches, down_state, up_state, gains, w_value, w_out,
        final_gain.reshape(1, D), lm_head, teacher_logits,
    )
    whole = (down, up, logits, divergence)
    down, up, logits, divergence = pl.pallas_call(
        hand_over,
        out_shape=tuple(jax.ShapeDtypeStruct(one.shape, one.dtype) for one in whole),
        in_specs=[vmem] * 4,
        out_specs=(vmem,) * 4,
        compiler_params=pltpu.CompilerParams(vmem_limit_bytes=VMEM_LIMIT),
        name="hand_over",
    )(*whole)
    return (down, up, logits, divergence.reshape(TICKS * MB))


def solution(mesh):
    placed = (
        P(None, "fsdp", None),
        P("segment", "fsdp", None),
        P("segment", "fsdp", None),
        P("segment", None, None),
        P("segment", None, None, "fsdp"),
        P("segment", None, "fsdp", None),
        P(),
        P(None, ("segment", "fsdp")),
        P(None, ("segment", "fsdp")),
    )
    return jax.shard_map(
        local,
        mesh=mesh,
        in_specs=placed,
        out_specs=(
            P("segment", "fsdp", None),
            P("segment", "fsdp", None),
            P(None, ("segment", "fsdp")),
            P(),
        ),
        check_vma=False,
    )
```
